256 devices in a mesh: section: 16 (over z, x_lo), dp: 16 (over y, x_hi, core).
Axes of the slice: x: 4 (x_hi: 2, x_lo: 2; x = x_hi * 2 + x_lo), y: 4, z: 8, core: 2. Of those that a mesh axis runs over, the one named last changes fastest.
Arguments:
- block_arguments: bfloat16 [2, 16, 2048, 2048], P(None, 'dp', 'section'), may hold values from -6 to 6
- incoming_batches: bfloat16 [2, 16, 128, 2048], P(None, 'dp'), may hold values from -6 to 6
- output_adjoints: bfloat16 [2, 16, 2048, 2048], P(None, 'dp', 'section'), may hold values from -0.0625 to 0.0625
- objective_adjoints: bfloat16 [2, 16, 128, 2048], P(None, 'dp'), may hold values from -0.0625 to 0.0625
- kept_block_arguments: bfloat16 [2, 2, 16, 2048, 2048], P(None, None, 'dp', 'section'), may hold values from -6 to 6
- parameter_arrays: bfloat16 [16, 2048, 1536], P('section', 'dp'), may hold values from -0.125 to 0.125
Outputs:
- ahead_out: bfloat16 [2, 16, 2048, 2048], P(None, 'dp', 'section')
- section_grads: float32 [16, 2048, 1536], P('section', 'dp')
The draws below stay inside these ranges and needn't reach their ends.
All inputs are finite; a program needn't handle non-finite values.
Results may differ from the reference program's by a relative error of at most 0.013.
Values may be sent and summed in bfloat16 or wider, within the bound.
No kernel may reach another device: no remote copies, remote signals or barrier semaphores. Data moves between devices by JAX's collectives and lax.ppermute only.
A program may use at most 128 MiB of HBM per device.

```python
import jax
import jax.numpy as jnp
from jax import lax

HIDDEN_FEATURES = 2048
FF = 512
SMALL_BATCH_SPAN = 128
GRAD_ROWS = 8192
N_SECTION = 16
N_DP = 16


def block_scale(rng, dims, pieces, low, largest):
    level, own = 1.0, jax.random.fold_in(rng, 6)
    for dim, parts in pieces:
        steps = jnp.exp(jax.random.uniform(jax.random.fold_in(own, dim), (parts,), jnp.float32, low / len(pieces), largest / len(pieces)))
        level = level * jnp.repeat(steps, dims[dim] // parts).reshape([-1 if axis == dim else 1 for axis in range(len(dims))])
    return level


def gaussian(stream_key, extent, width, limit, shards=(), held_as=jnp.bfloat16):
    drawn = width * jax.random.normal(stream_key, extent, jnp.float32)
    if shards:
        drawn = drawn * block_scale(stream_key, extent, shards, -0.22, 0.18)
    return jnp.clip(drawn, -limit, limit).astype(held_as)


def setup_inputs(seed: int = 0) -> dict:
    arg_keys = jax.random.split(jax.random.key(seed), 7)
    block_arguments = gaussian(arg_keys[0], (2, N_DP, N_SECTION * SMALL_BATCH_SPAN, HIDDEN_FEATURES), 1.0, 6.0, ((1, 16), (2, 16)))
    incoming_batches = gaussian(arg_keys[1], (2, N_DP, SMALL_BATCH_SPAN, HIDDEN_FEATURES), 1.0, 6.0, ((1, 16),))
    output_adjoints = gaussian(arg_keys[2], (2, N_DP, N_SECTION * SMALL_BATCH_SPAN, HIDDEN_FEATURES), (1.0 / GRAD_ROWS ** 0.5), 0.0625, ((1, 16), (2, 16)))
    objective_adjoints = gaussian(arg_keys[3], (2, N_DP, SMALL_BATCH_SPAN, HIDDEN_FEATURES), (1.0 / GRAD_ROWS ** 0.5), 0.0625, ((1, 16),))
    kept_block_arguments = gaussian(arg_keys[4], (2, 2, N_DP, N_SECTION * SMALL_BATCH_SPAN, HIDDEN_FEATURES), 1.0, 6.0, ((2, 16), (3, 16)))
    parameter_arrays = gaussian(arg_keys[5], (N_SECTION, HIDDEN_FEATURES, 3 * FF), HIDDEN_FEATURES ** -0.5, 0.125, ((0, 16), (1, 16)))
    return {"block_arguments": block_arguments, "incoming_batches": incoming_batches, "output_adjoints": output_adjoints, "objective_adjoints": objective_adjoints, "kept_block_arguments": kept_block_arguments, "parameter_arrays": parameter_arrays}


def normalize(row_block):
    values = row_block.astype(jnp.float32)
    inverse = lax.rsqrt(lax.optimization_barrier(jnp.mean(values * values, axis=-1, keepdims=True)) + 1e-06)
    return (values, inverse, (values * inverse).astype(jnp.bfloat16))

def section_forward(row_block, matrix):
    hidden_width = matrix.shape[1] // 3
    values, inverse, normed = normalize(row_block)
    projected = jnp.dot(normed, matrix[:, :2 * hidden_width], preferred_element_type=jnp.float32)
    gate_part = projected[:, :hidden_width]
    up_part = projected[:, hidden_width:]
    hidden = (gate_part * jax.nn.sigmoid(gate_part) * up_part).astype(jnp.bfloat16)
    branch = lax.dot_general(hidden, matrix[:, 2 * hidden_width:], (((1,), (1,)), ((), ())), preferred_element_type=jnp.float32)
    return (values + branch).astype(jnp.bfloat16)

def section_reverse_pass(row_block, cotangent, matrix, with_input):
    hidden_width = matrix.shape[1] // 3
    values, inverse, normed = normalize(row_block)
    projected = jnp.dot(normed, matrix[:, :2 * hidden_width], preferred_element_type=jnp.float32)
    gate_part = projected[:, :hidden_width]
    up_part = projected[:, hidden_width:]
    sigmoid_gate = jax.nn.sigmoid(gate_part)
    silu_gate = gate_part * sigmoid_gate
    hidden = (silu_gate * up_part).astype(jnp.bfloat16)
    hidden_grad = jnp.dot(cotangent, matrix[:, 2 * hidden_width:], preferred_element_type=jnp.float32)
    projected_grad = jnp.concatenate([hidden_grad * up_part * sigmoid_gate * (1.0 + gate_part * (1.0 - sigmoid_gate)), hidden_grad * silu_gate], axis=1).astype(jnp.bfloat16)
    inward_grad = lax.dot_general(normed, projected_grad, (((0,), (0,)), ((), ())), preferred_element_type=jnp.float32)
    outward_grad = lax.dot_general(cotangent, hidden, (((0,), (0,)), ((), ())), preferred_element_type=jnp.float32)
    weight_term = jnp.concatenate([inward_grad, outward_grad], axis=1)
    if not with_input:
        return (weight_term, None)
    normed_grad = lax.dot_general(projected_grad, matrix[:, :2 * hidden_width], (((1,), (1,)), ((), ())), preferred_element_type=jnp.float32)
    inner_sum = lax.optimization_barrier(jnp.mean(normed_grad * values, axis=-1, keepdims=True))
    input_grad = cotangent.astype(jnp.float32) + inverse * normed_grad - values * inverse * inverse * inverse * inner_sum
    return (weight_term, input_grad.astype(jnp.bfloat16))

def replica_sums(first_rows, first_cot, second_rows, second_cot, matrix):

    def add_one(total, items):
        rows_one, cot_one, rows_two, cot_two = items
        term_one, discarded_value = section_reverse_pass(rows_one, cot_one, matrix, False)
        term_two, discarded_second = section_reverse_pass(rows_two, cot_two, matrix, False)
        rounded = lax.optimization_barrier((term_one + term_two).astype(jnp.bfloat16))
        return (total + rounded.astype(jnp.float32), None)
    start = jnp.zeros((HIDDEN_FEATURES, 3 * FF), jnp.float32)
    total, discarded_value = lax.scan(add_one, start, (first_rows, first_cot, second_rows, second_cot))
    return total

def reference(block_arguments, incoming_batches, output_adjoints, objective_adjoints, kept_block_arguments, parameter_arrays):
    segment_sequence_catalog = N_SECTION
    first_in = block_arguments.reshape(2, N_DP, segment_sequence_catalog, SMALL_BATCH_SPAN, HIDDEN_FEATURES)
    first_cot = output_adjoints.reshape(2, N_DP, segment_sequence_catalog, SMALL_BATCH_SPAN, HIDDEN_FEATURES)
    retained_intermediates = kept_block_arguments.reshape(2, 2, N_DP, segment_sequence_catalog, SMALL_BATCH_SPAN, HIDDEN_FEATURES)
    matrices = jnp.stack([parameter_arrays, parameter_arrays[::-1]])

    def flatten_rows(rows):
        return rows.reshape(N_DP * SMALL_BATCH_SPAN, HIDDEN_FEATURES)

    def shaped(rows):
        return rows.reshape(N_DP, SMALL_BATCH_SPAN, HIDDEN_FEATURES)

    def first_pass(position):
        forward_list = []
        back_list = []
        for course in range(2):
            matrix = matrices[course, position]
            forward_list.append(shaped(section_forward(flatten_rows(first_in[course, :, position]), matrix)))
            discarded_value, back_rows = section_reverse_pass(flatten_rows(retained_intermediates[course, 0, :, position]), flatten_rows(first_cot[course, :, position]), matrix, True)
            back_list.append(shaped(back_rows))
        return (jnp.stack(forward_list), jnp.stack(back_list))
    first_out, returned = lax.map(first_pass, jnp.arange(segment_sequence_catalog))
    down_in = jnp.concatenate([incoming_batches[0][None], first_out[:-1, 0]], axis=0)
    up_in = jnp.concatenate([first_out[1:, 1], incoming_batches[1][None]], axis=0)
    descending_adjoint = jnp.concatenate([returned[1:, 0], objective_adjoints[0][None]], axis=0)
    ascending_adjoint = jnp.concatenate([objective_adjoints[1][None], returned[:-1, 1]], axis=0)
    second_in = jnp.stack([down_in, up_in], axis=1)
    second_cot = jnp.stack([descending_adjoint, ascending_adjoint], axis=1)

    def second_pass(position):
        forward_list = []
        sum_list = []
        for course in range(2):
            matrix = matrices[course, position]
            forward_list.append(shaped(section_forward(flatten_rows(second_in[position, course]), matrix)))
            sum_list.append(replica_sums(retained_intermediates[course, 0, :, position], first_cot[course, :, position], retained_intermediates[course, 1, :, position], second_cot[position, course], matrix))
        return (jnp.stack(forward_list), jnp.stack(sum_list))
    later_out, totals = lax.map(second_pass, jnp.arange(segment_sequence_catalog))
    section_grads = totals[:, 0] + totals[::-1, 1]
    ahead_out = jnp.transpose(later_out, (1, 2, 0, 3, 4)).reshape(2, N_DP, segment_sequence_catalog * SMALL_BATCH_SPAN, HIDDEN_FEATURES)
    return (ahead_out, section_grads)
```

```python
import jax
import jax.numpy as jnp
from jax import lax
from jax.sharding import PartitionSpec as P

N_Y, N_XH, N_CORE = 4, 2, 2
BOTH = ("section", "dp")


def dp_index(y, xh, core):
    return (y % N_Y) * (N_XH * N_CORE) + (xh % N_XH) * N_CORE + core % N_CORE


def dp_coords(index):
    return index // (N_XH * N_CORE), index // N_CORE % N_XH, index % N_CORE


def dp_shift(block, dy=0, dxh=0, dcore=0):
    route = []
    for index in range(N_Y * N_XH * N_CORE):
        y, xh, core = dp_coords(index)
        route.append((index, dp_index(y + dy, xh + dxh, core + dcore)))
    return lax.ppermute(block, "dp", route)


def flip_xh(index):
    y, xh, core = dp_coords(index)
    return dp_index(y, 1 - xh, core)


def mirror(block):
    n, m = lax.axis_size("section"), lax.axis_size("dp")
    route = [(p * m + d, (n - 1 - p) * m + flip_xh(d)) for p in range(n) for d in range(m)]
    return lax.ppermute(block, BOTH, route)


def relay(block, step):
    n, m = lax.axis_size("section"), lax.axis_size("dp")
    route = []
    for p in range(n):
        for d in range(m):
            q = p + step
            wraps = q < 0 or q >= n
            route.append((p * m + d, q % n * m + (flip_xh(d) if wraps else d)))
    return lax.ppermute(block, BOTH, route)


def gather_matrix(shard, y, xh, core):
    rows, width = shard.shape
    other = dp_shift(shard, dxh=1)
    groups = [(0, 0, shard), (0, 1, other)]
    near = {}
    for dxh, block in ((0, shard), (1, other)):
        near[1, dxh] = dp_shift(block, dy=-1)
        near[3, dxh] = dp_shift(block, dy=1)
        groups += [(1, dxh, near[1, dxh]), (3, dxh, near[3, dxh])]
    groups.append((2, 0, dp_shift(near[1, 0], dy=-1)))
    groups.append((2, 1, dp_shift(near[3, 1], dy=1)))
    matrix = jnp.zeros((N_Y * N_XH * N_CORE, rows, width), shard.dtype)
    for dy, dxh, block in groups:
        across = dp_shift(block, dcore=1)
        place = dp_index(y + dy, xh + dxh, 0)
        matrix = lax.dynamic_update_slice(matrix, block[None], (place + core, 0, 0))
        matrix = lax.dynamic_update_slice(matrix, across[None], (place + 1 - core, 0, 0))
    return matrix.reshape(N_Y * N_XH * N_CORE * rows, width)


def normalize(row_block):
    values = row_block.astype(jnp.float32)
    inverse = lax.rsqrt(jnp.mean(values * values, axis=-1, keepdims=True) + 1e-06)
    return values, inverse, (values * inverse).astype(jnp.bfloat16)


def project(row_block, matrix):
    width = matrix.shape[1] // 3
    values, inverse, normed = normalize(row_block)
    projected = jnp.dot(normed, matrix[:, : 2 * width], preferred_element_type=jnp.float32)
    return values, inverse, normed, projected[:, :width], projected[:, width:]


def section_forward(row_block, matrix):
    width = matrix.shape[1] // 3
    values, _, _, gate, up = project(row_block, matrix)
    hidden = (gate * jax.nn.sigmoid(gate) * up).astype(jnp.bfloat16)
    branch = lax.dot_general(
        hidden, matrix[:, 2 * width :], (((1,), (1,)), ((), ())), preferred_element_type=jnp.float32
    )
    return (values + branch).astype(jnp.bfloat16)


def hidden_of(gate, up):
    return (gate * jax.nn.sigmoid(gate) * up).astype(jnp.bfloat16)


def projected_grad_of(cotangent, gate, up, matrix):
    width = matrix.shape[1] // 3
    hidden_grad = jnp.dot(cotangent, matrix[:, 2 * width :], preferred_element_type=jnp.float32)
    sigmoid = jax.nn.sigmoid(gate)
    return jnp.concatenate(
        [
            hidden_grad * up * sigmoid * (1.0 + gate * (1.0 - sigmoid)),
            hidden_grad * (gate * sigmoid),
        ],
        axis=1,
    ).astype(jnp.bfloat16)


def input_grad_of(cotangent, values, inverse, projected_grad, matrix):
    width = matrix.shape[1] // 3
    normed_grad = lax.dot_general(
        projected_grad,
        matrix[:, : 2 * width],
        (((1,), (1,)), ((), ())),
        preferred_element_type=jnp.float32,
    )
    inner = jnp.mean(normed_grad * values, axis=-1, keepdims=True)
    return (
        cotangent.astype(jnp.float32)
        + inverse * normed_grad
        - values * inverse * inverse * inverse * inner
    ).astype(jnp.bfloat16)


def columns_of_core(rows, core):
    tokens, features = rows.shape
    blocks = rows.reshape(tokens, N_Y * N_XH, N_CORE, features // (N_Y * N_XH * N_CORE))
    picked = lax.dynamic_index_in_dim(blocks, core, axis=2, keepdims=False)
    return picked.reshape(tokens, features // N_CORE)


def over_tokens(rows, grads):
    return lax.dot_general(rows, grads, (((0,), (0,)), ((), ())), preferred_element_type=jnp.float32)


def at(blocks, index, axis=0):
    return lax.dynamic_index_in_dim(blocks, index, axis=axis, keepdims=False)


def core_sum(rows, grads, core):
    away = over_tokens(columns_of_core(rows, 1 - core), grads).astype(jnp.bfloat16)
    arrived = dp_shift(away, dcore=1)
    own = over_tokens(columns_of_core(rows, core), grads)
    total = (own + arrived.astype(jnp.float32)).astype(jnp.bfloat16)
    return total.reshape(N_Y, N_XH, -1, grads.shape[1])


def sum_along_y(blocks, y):
    total = at(blocks, y).astype(jnp.float32)
    for dy in (1, 2, 3):
        total = total + dp_shift(at(blocks, (y + dy) % N_Y), dy=dy).astype(jnp.float32)
    return total


def sum_y_first(blocks, y, xh):
    partial = sum_along_y(blocks, y)
    arrived = dp_shift(at(partial, 1 - xh).astype(jnp.bfloat16), dxh=1)
    return at(partial, xh) + arrived.astype(jnp.float32)


def sum_xh_first(blocks, y, xh):
    arrived = dp_shift(at(blocks, 1 - xh, axis=1), dxh=1)
    partial = at(blocks, xh, axis=1).astype(jnp.float32) + arrived.astype(jnp.float32)
    return sum_along_y(partial.astype(jnp.bfloat16), y)


def on_device(
    block_arguments,
    incoming_batches,
    output_adjoints,
    objective_adjoints,
    kept_block_arguments,
    parameter_arrays,
):
    section = lax.axis_index("section")
    first = section == 0
    last = section == lax.axis_size("section") - 1
    y, xh, core = dp_coords(lax.axis_index("dp"))
    span = block_arguments.shape[2]

    def joined(pair):
        return jnp.concatenate(pair, axis=0)

    kept_first = joined([kept_block_arguments[0, 0, 0], mirror(kept_block_arguments[1, 0, 0])])
    cot_first = joined([output_adjoints[0, 0], mirror(output_adjoints[1, 0])])
    rows_first = joined([block_arguments[0, 0], mirror(block_arguments[1, 0])])
    kept_second = joined([kept_block_arguments[0, 1, 0], mirror(kept_block_arguments[1, 1, 0])])
    matrix = gather_matrix(parameter_arrays[0], y, xh, core)

    values, inverse, normed_first, gate, up = project(kept_first, matrix)
    hidden_first = hidden_of(gate, up)
    grad_first = projected_grad_of(cot_first, gate, up, matrix)
    back = input_grad_of(cot_first, values, inverse, grad_first, matrix)
    back = joined([back[:span], jnp.where(first, objective_adjoints[1, 0], back[span:])])
    back_arrived = relay(back, -1)

    ahead = section_forward(rows_first, matrix)
    ahead = joined([ahead[:span], jnp.where(last, incoming_batches[1, 0], ahead[span:])])
    ahead_arrived = relay(ahead, 1)

    _, _, normed_second, gate, up = project(kept_second, matrix)
    hidden_second = hidden_of(gate, up)

    cot_second = joined(
        [jnp.where(last, objective_adjoints[0, 0], back_arrived[:span]), back_arrived[span:]]
    )
    outward = core_sum(joined([cot_first, cot_second]), joined([hidden_first, hidden_second]), core)
    grad_second = projected_grad_of(cot_second, gate, up, matrix)
    inward = core_sum(joined([normed_first, normed_second]), joined([grad_first, grad_second]), core)
    outward_rows = sum_xh_first(outward, y, xh)
    inward_rows = sum_y_first(inward, y, xh)

    rows_second = joined(
        [jnp.where(first, incoming_batches[0, 0], ahead_arrived[:span]), ahead_arrived[span:]]
    )
    ahead_second = section_forward(rows_second, matrix)
    ahead_out = jnp.stack([ahead_second[:span], mirror(ahead_second[span:])])[:, None]
    return ahead_out, jnp.concatenate([inward_rows, outward_rows], axis=1)[None]


def solution(mesh):
    in_specs = (
        P(None, "dp", "section", None),
        P(None, "dp", None, None),
        P(None, "dp", "section", None),
        P(None, "dp", None, None),
        P(None, None, "dp", "section", None),
        P("section", "dp", None),
    )
    out_specs = (P(None, "dp", "section", None), P("section", "dp", None))
    return jax.shard_map(
        on_device, mesh=mesh, in_specs=in_specs, out_specs=out_specs, check_vma=False
    )
```

```python
import jax
import jax.numpy as jnp
from jax import lax
from jax.sharding import PartitionSpec as P

N_Y, N_XH, N_CORE = 4, 2, 2
BOTH = ("section", "dp")


def dp_index(y, xh, core):
    return (y & 3) << 2 | (xh & 1) << 1 | core & 1


def dp_coords(index):
    return index >> 2, index >> 1 & 1, index & 1


def dp_shift(block, dy=0, dxh=0, dcore=0):
    route = []
    for index in range(N_Y * N_XH * N_CORE):
        y, xh, core = dp_coords(index)
        route.append((index, dp_index(y + dy, xh + dxh, core + dcore)))
    return lax.ppermute(block, "dp", route)


def flip_xh(index):
    y, xh, core = dp_coords(index)
    return dp_index(y, 1 - xh, core)


def mirror(block):
    n, m = lax.axis_size("section"), lax.axis_size("dp")
    route = [(p * m + d, (n - 1 - p) * m + flip_xh(d)) for p in range(n) for d in range(m)]
    return lax.ppermute(block, BOTH, route)


def relay(block, step):
    n, m = lax.axis_size("section"), lax.axis_size("dp")
    route = []
    for p in range(n):
        for d in range(m):
            q = p + step
            wraps = q < 0 or q >= n
            route.append((p * m + d, q % n * m + (flip_xh(d) if wraps else d)))
    return lax.ppermute(block, BOTH, route)


def after(block, *earlier):
    return lax.optimization_barrier((block, *earlier))[0]


def gather_half(shard, y, xh):
    rows, width = shard.shape
    other = dp_shift(shard, dxh=1)
    up, down = dp_shift(shard, dy=-1), dp_shift(shard, dy=1)
    up_other, down_other = dp_shift(other, dy=-1), dp_shift(other, dy=1)
    far = dp_shift(up, dy=-1)
    far_other = dp_shift(down_other, dy=1)
    half = jnp.zeros((N_Y * N_XH, rows, width), shard.dtype)
    for dy, dxh, block in (
        (0, 0, shard),
        (0, 1, other),
        (1, 0, up),
        (3, 0, down),
        (1, 1, up_other),
        (3, 1, down_other),
        (2, 0, far),
        (2, 1, far_other),
    ):
        place = (y + dy & 3) << 1 | xh ^ dxh
        half = lax.dynamic_update_slice(half, block[None], (place, 0, 0))
    return half, other


def whole_matrix(half, core):
    blocks, rows, width = half.shape
    across = dp_shift(half, dcore=1)
    even = core == 0
    pair = jnp.stack([jnp.where(even, half, across), jnp.where(even, across, half)], axis=1)
    return pair.reshape(N_CORE * blocks * rows, width)


def normalize(row_block):
    values = row_block.astype(jnp.float32)
    inverse = lax.rsqrt(jnp.mean(values * values, axis=-1, keepdims=True) + 1e-06)
    return values, inverse, (values * inverse).astype(jnp.bfloat16)


def project(row_block, matrix):
    width = matrix.shape[1] // 3
    values, inverse, normed = normalize(row_block)
    projected = jnp.dot(normed, matrix[:, : 2 * width], preferred_element_type=jnp.float32)
    return values, inverse, normed, projected[:, :width], projected[:, width:]


def section_forward(row_block, matrix):
    width = matrix.shape[1] // 3
    values, _, _, gate, up = project(row_block, matrix)
    hidden = (gate * jax.nn.sigmoid(gate) * up).astype(jnp.bfloat16)
    branch = lax.dot_general(
        hidden, matrix[:, 2 * width :], (((1,), (1,)), ((), ())), preferred_element_type=jnp.float32
    )
    return (values + branch).astype(jnp.bfloat16)


def hidden_of(gate, up):
    return (gate * jax.nn.sigmoid(gate) * up).astype(jnp.bfloat16)


def projected_grad_of(cotangent, gate, up, matrix):
    width = matrix.shape[1] // 3
    hidden_grad = jnp.dot(cotangent, matrix[:, 2 * width :], preferred_element_type=jnp.float32)
    sigmoid = jax.nn.sigmoid(gate)
    return jnp.concatenate(
        [
            hidden_grad * up * sigmoid * (1.0 + gate * (1.0 - sigmoid)),
            hidden_grad * (gate * sigmoid),
        ],
        axis=1,
    ).astype(jnp.bfloat16)


def input_grad_of(cotangent, values, inverse, projected_grad, matrix):
    width = matrix.shape[1] // 3
    normed_grad = lax.dot_general(
        projected_grad,
        matrix[:, : 2 * width],
        (((1,), (1,)), ((), ())),
        preferred_element_type=jnp.float32,
    )
    inner = jnp.mean(normed_grad * values, axis=-1, keepdims=True)
    return (
        cotangent.astype(jnp.float32)
        + inverse * normed_grad
        - values * inverse * inverse * inverse * inner
    ).astype(jnp.bfloat16)


def columns_of_core(rows, core):
    tokens, features = rows.shape
    blocks = rows.reshape(tokens, N_Y * N_XH, N_CORE, features // (N_Y * N_XH * N_CORE))
    picked = lax.dynamic_index_in_dim(blocks, core, axis=2, keepdims=False)
    return picked.reshape(tokens, features // N_CORE)


def over_tokens(rows, grads):
    return lax.dot_general(rows, grads, (((0,), (0,)), ((), ())), preferred_element_type=jnp.float32)


def at(blocks, index, axis=0):
    return lax.dynamic_index_in_dim(blocks, index, axis=axis, keepdims=False)


def core_sum(rows, grads, core):
    away = over_tokens(columns_of_core(rows, 1 - core), grads).astype(jnp.bfloat16)
    arrived = dp_shift(away, dcore=1)
    own = over_tokens(columns_of_core(rows, core), grads)
    total = (own + arrived.astype(jnp.float32)).astype(jnp.bfloat16)
    return total.reshape(N_Y, N_XH, -1, grads.shape[1])


def send_along_y(blocks, y):
    return [dp_shift(at(blocks, y + dy & 3), dy=dy) for dy in (1, 2, 3)]


def sum_along_y(blocks, arrived, y):
    total = at(blocks, y).astype(jnp.float32)
    for block in arrived:
        total = total + block.astype(jnp.float32)
    return total


def sum_over_xh(blocks, xh, axis):
    arrived = dp_shift(at(blocks, 1 - xh, axis).astype(jnp.bfloat16), dxh=1)
    return at(blocks, xh, axis).astype(jnp.float32) + arrived.astype(jnp.float32)


def on_device(
    block_arguments,
    incoming_batches,
    output_adjoints,
    objective_adjoints,
    kept_block_arguments,
    parameter_arrays,
):
    section = lax.axis_index("section")
    first = section == 0
    last = section == lax.axis_size("section") - 1
    y, xh, core = dp_coords(lax.axis_index("dp"))
    span = block_arguments.shape[2]

    def joined(pair):
        return jnp.concatenate(pair, axis=0)

    half, over_x = gather_half(parameter_arrays[0], y, xh)
    kept_arrived = mirror(after(kept_block_arguments[1, 0, 0], over_x))
    cot_arrived = mirror(after(output_adjoints[1, 0], over_x))
    half, kept_arrived, cot_arrived = lax.optimization_barrier((half, kept_arrived, cot_arrived))
    rows_arrived = mirror(after(block_arguments[1, 0], kept_arrived))
    matrix = whole_matrix(half, core)
    kept_first = joined([kept_block_arguments[0, 0, 0], kept_arrived])
    cot_first = joined([output_adjoints[0, 0], cot_arrived])

    values, inverse, normed_first, gate, up = project(kept_first, matrix)
    hidden_first = hidden_of(gate, up)
    grad_first = projected_grad_of(cot_first, gate, up, matrix)
    back = input_grad_of(cot_first, values, inverse, grad_first, matrix)
    back = joined([back[:span], jnp.where(first, objective_adjoints[1, 0], back[span:])])
    back_arrived = relay(back, -1)

    rows_arrived = after(rows_arrived, back)
    kept_later = mirror(after(kept_block_arguments[1, 1, 0], rows_arrived))
    rows_first = joined([block_arguments[0, 0], rows_arrived])
    kept_second = joined([kept_block_arguments[0, 1, 0], kept_later])
    ahead = section_forward(rows_first, matrix)
    ahead = joined([ahead[:span], jnp.where(last, incoming_batches[1, 0], ahead[span:])])
    ahead_arrived = relay(after(ahead, back_arrived), 1)

    _, _, normed_second, gate, up = project(kept_second, matrix)
    hidden_second = hidden_of(gate, up)
    back_arrived = after(back_arrived, hidden_second, ahead)

    cot_second = joined(
        [jnp.where(last, objective_adjoints[0, 0], back_arrived[:span]), back_arrived[span:]]
    )
    outward = core_sum(joined([cot_first, cot_second]), joined([hidden_first, hidden_second]), core)
    grad_second = projected_grad_of(cot_second, gate, up, matrix)
    inward = core_sum(joined([normed_first, normed_second]), joined([grad_first, grad_second]), core)
    outward = sum_over_xh(outward, xh, 1).astype(jnp.bfloat16)
    inward = sum_along_y(inward, send_along_y(inward, y), y)
    inward, outward, ahead_arrived = lax.optimization_barrier((inward, outward, ahead_arrived))
    inward_rows = sum_over_xh(inward, xh, 0)
    outward_rows = sum_along_y(outward, send_along_y(outward, y), y)

    rows_second = joined(
        [jnp.where(first, incoming_batches[0, 0], ahead_arrived[:span]), ahead_arrived[span:]]
    )
    ahead_second = section_forward(rows_second, matrix)
    ahead_out = jnp.stack([ahead_second[:span], mirror(ahead_second[span:])])[:, None]
    return ahead_out, jnp.concatenate([inward_rows, outward_rows], axis=1)[None]


def solution(mesh):
    in_specs = (
        P(None, "dp", "section", None),
        P(None, "dp", None, None),
        P(None, "dp", "section", None),
        P(None, "dp", None, None),
        P(None, None, "dp", "section", None),
        P("section", "dp", None),
    )
    out_specs = (P(None, "dp", "section", None), P("section", "dp", None))
    return jax.shard_map(
        on_device, mesh=mesh, in_specs=in_specs, out_specs=out_specs, check_vma=False
    )
```

```python
import jax
import jax.numpy as jnp
from jax import lax
from jax.sharding import PartitionSpec as P

N_Y, N_XH, N_CORE = 4, 2, 2
ROWS = 128


def dp_index(y, xh, core):
    return (y & 3) << 2 | (xh & 1) << 1 | core & 1


def dp_coords(index):
    return index >> 2, index >> 1 & 1, index & 1


def dp_shift(block, dy=0, dxh=0, dcore=0):
    route = []
    for index in range(N_Y * N_XH * N_CORE):
        y, xh, core = dp_coords(index)
        route.append((index, dp_index(y + dy, xh + dxh, core + dcore)))
    return lax.ppermute(block, "dp", route)


def mirror(block):
    n = lax.axis_size("section")
    return lax.ppermute(block, "section", [(p, n - 1 - p) for p in range(n)])


def relay(block, step):
    n = lax.axis_size("section")
    return lax.ppermute(block, "section", [(p, p + step) for p in range(n) if 0 <= p + step < n])


def first_hops(shard):
    return dp_shift(shard, dy=-1), dp_shift(shard, dy=1)


def gather_half(shard, other, hops, y, xh, earlier):
    rows, width = shard.shape
    up, down = hops
    up_other, down_other = first_hops(other)
    up, down_other, earlier = lax.optimization_barrier((up, down_other, earlier))
    far = dp_shift(up, dy=-1)
    far_other = dp_shift(down_other, dy=1)
    half = jnp.zeros((N_Y * N_XH, rows, width), shard.dtype)
    for dy, dxh, block in (
        (0, 0, shard),
        (0, 1, other),
        (1, 0, up),
        (3, 0, down),
        (1, 1, up_other),
        (3, 1, down_other),
        (2, 0, far),
        (2, 1, far_other),
    ):
        place = (y + dy & 3) << 1 | xh ^ dxh
        half = lax.dynamic_update_slice(half, block[None], (place, 0, 0))
    return half, earlier


def interleaved(half, across, core):
    blocks, rows, width = half.shape
    even = core == 0
    pair = jnp.stack([jnp.where(even, half, across), jnp.where(even, across, half)], axis=1)
    return pair.reshape(N_CORE * blocks * rows, width)


def normalize(row_block):
    values = row_block.astype(jnp.float32)
    inverse = lax.rsqrt(jnp.mean(values * values, axis=-1, keepdims=True) + 1e-06)
    return values, inverse, (values * inverse).astype(jnp.bfloat16)


def gate_and_up(normed, matrix):
    width = matrix.shape[1] // 3
    projected = jnp.dot(normed, matrix[:, : 2 * width], preferred_element_type=jnp.float32)
    return projected[:, :width], projected[:, width:]


def project(row_block, matrix):
    values, inverse, normed = normalize(row_block)
    return values, inverse, normed, *gate_and_up(normed, matrix)


def section_forward(row_block, matrix):
    width = matrix.shape[1] // 3
    values, _, _, gate, up = project(row_block, matrix)
    hidden = (gate * jax.nn.sigmoid(gate) * up).astype(jnp.bfloat16)
    branch = lax.dot_general(
        hidden, matrix[:, 2 * width :], (((1,), (1,)), ((), ())), preferred_element_type=jnp.float32
    )
    return (values + branch).astype(jnp.bfloat16)


def hidden_of(gate, up):
    return (gate * jax.nn.sigmoid(gate) * up).astype(jnp.bfloat16)


def projected_grad_of(cotangent, gate, up, matrix):
    width = matrix.shape[1] // 3
    hidden_grad = jnp.dot(cotangent, matrix[:, 2 * width :], preferred_element_type=jnp.float32)
    sigmoid = jax.nn.sigmoid(gate)
    return jnp.concatenate(
        [
            hidden_grad * up * sigmoid * (1.0 + gate * (1.0 - sigmoid)),
            hidden_grad * (gate * sigmoid),
        ],
        axis=1,
    ).astype(jnp.bfloat16)


def input_grad_of(cotangent, values, inverse, projected_grad, matrix):
    width = matrix.shape[1] // 3
    normed_grad = lax.dot_general(
        projected_grad,
        matrix[:, : 2 * width],
        (((1,), (1,)), ((), ())),
        preferred_element_type=jnp.float32,
    )
    inner = jnp.mean(normed_grad * values, axis=-1, keepdims=True)
    return (
        cotangent.astype(jnp.float32)
        + inverse * normed_grad
        - values * inverse * inverse * inverse * inner
    ).astype(jnp.bfloat16)


def over_tokens(rows, grads):
    return lax.dot_general(rows, grads, (((0,), (0,)), ((), ())), preferred_element_type=jnp.float32)


def at(blocks, index, axis=0):
    return lax.dynamic_index_in_dim(blocks, index, axis=axis, keepdims=False)


def split_by_core(grad, core):
    halves = grad.reshape(-1, N_CORE, ROWS, grad.shape[1])
    return at(halves, core, 1), at(halves, 1 - core, 1)


def core_sum(own, arrived):
    sums = [a.astype(jnp.float32) + b.astype(jnp.float32) for a, b in zip(own, arrived)]
    total = jnp.concatenate(sums, axis=2).astype(jnp.bfloat16)
    return total.reshape(N_Y, N_XH, *total.shape[1:])


def parts_along_y(blocks, y):
    return [at(blocks, y + dy & 3) for dy in (1, 3, 2)]


def send_along_y(parts):
    return [dp_shift(part, dy=dy) for dy, part in zip((1, 3, 2), parts)]


def sum_along_y(blocks, arrived, y):
    total = at(blocks, y).astype(jnp.float32)
    for block in arrived:
        total = total + block.astype(jnp.float32)
    return total


def sum_over_xh(blocks, xh, axis):
    arrived = dp_shift(at(blocks, 1 - xh, axis).astype(jnp.bfloat16), dxh=1)
    return at(blocks, xh, axis).astype(jnp.float32) + arrived.astype(jnp.float32)


def on_device(
    block_arguments,
    incoming_batches,
    output_adjoints,
    objective_adjoints,
    kept_block_arguments,
    parameter_arrays,
):
    section = lax.axis_index("section")
    first = section == 0
    last = section == lax.axis_size("section") - 1
    y, xh, core = dp_coords(lax.axis_index("dp"))

    def joined(pair):
        return jnp.concatenate(pair, axis=0)

    ends = ((first, last), (last, first))
    tie = lax.optimization_barrier

    def first_tick(cotangent, matrix, norm):
        values, inverse, normed = norm
        gate, up = gate_and_up(normed, matrix)
        grad = projected_grad_of(cotangent, gate, up, matrix)
        back = input_grad_of(cotangent, values, inverse, grad, matrix)
        return (normed, grad, cotangent, hidden_of(gate, up)), back

    def second_tick(way, matrix, projected, back_arrived):
        normed, gate, up = projected
        cotangent = jnp.where(ends[way][1], objective_adjoints[way, 0], back_arrived)
        return normed, projected_grad_of(cotangent, gate, up, matrix), cotangent, hidden_of(gate, up)

    def rows_by_core(pieces_first, pieces_second):
        normed, grad, cotangent, hidden = (joined(pair) for pair in zip(pieces_first, pieces_second))
        inward = split_by_core(over_tokens(normed, grad).astype(jnp.bfloat16), core)
        outward = [
            split_by_core(over_tokens(cot, hidden).astype(jnp.bfloat16), core)
            for cot in jnp.split(cotangent, 2, axis=1)
        ]
        own, away = ([inward[k], joined([part[k] for part in outward])] for k in (0, 1))
        return own, away

    def core_swap(blocks):
        return [dp_shift(block, dcore=1) for block in blocks]

    def last_rows(way, ahead_arrived):
        return jnp.where(ends[way][0], incoming_batches[way, 0], ahead_arrived)

    own_shard = parameter_arrays[0]
    mirror_shard = mirror(own_shard)
    half_down, mirror_shard = gather_half(
        own_shard, dp_shift(own_shard, dxh=1), first_hops(own_shard), y, xh, mirror_shard
    )
    norm_down, norm_up = (normalize(kept_block_arguments[way, 0, 0]) for way in (0, 1))
    half_down, mirror_other, norm_down, cot_down, block_down = tie(
        (half_down, dp_shift(mirror_shard, dxh=1), norm_down, output_adjoints[0, 0], block_arguments[0, 0])
    )
    matrix_down = interleaved(half_down, dp_shift(half_down, dcore=1), core)
    down_first, back_down = first_tick(cot_down, matrix_down, norm_down)
    half_up, hidden_down = gather_half(
        mirror_shard, mirror_other, first_hops(mirror_shard), y, xh, down_first[3]
    )
    down_first = (*down_first[:3], hidden_down)
    back_down_arrived = relay(back_down, -1)
    across_up = dp_shift(half_up, dcore=1)
    ahead_down = section_forward(block_down, matrix_down)
    _, _, *projected_down = project(kept_block_arguments[0, 1, 0], matrix_down)
    back_down_arrived, ahead_down, projected_down = tie((back_down_arrived, ahead_down, projected_down))
    ahead_down_arrived = relay(ahead_down, 1)
    down_second = second_tick(0, matrix_down, projected_down, back_down_arrived)
    own_down, away_down = rows_by_core(down_first, down_second)

    half_up, across_up, away_down = tie((half_up, across_up, away_down))
    away_down_arrived = core_swap(away_down)
    matrix_up = interleaved(half_up, across_up, core)
    up_first, back_up = first_tick(output_adjoints[1, 0], matrix_up, norm_up)
    back_up, away_down_arrived = tie((back_up, away_down_arrived))
    back_up_arrived = relay(back_up, 1)
    total_down = core_sum(own_down, away_down_arrived)
    parts_down = parts_along_y(total_down, y)
    block_up, parts_down = tie((block_arguments[1, 0], parts_down))
    ahead_up = section_forward(block_up, matrix_up)
    _, _, *projected_up = project(kept_block_arguments[1, 1, 0], matrix_up)
    back_up_arrived, ahead_up, projected_up = tie((back_up_arrived, ahead_up, projected_up))
    ahead_up_arrived = relay(ahead_up, -1)
    up_second = second_tick(1, matrix_up, projected_up, back_up_arrived)
    own_up, away_up = rows_by_core(up_first, up_second)
    y_down = send_along_y(parts_down)
    away_up, y_down = tie((away_up, y_down))
    inward_up, outward_up = (core_sum([a], [b]) for a, b in zip(own_up, core_swap(away_up)))
    parts_up = parts_along_y(inward_up, y)
    outward_up = sum_over_xh(outward_up, xh, 1).astype(jnp.bfloat16)
    inward_up = sum_along_y(inward_up, send_along_y(parts_up), y)
    inward_up, outward_up = tie((inward_up, outward_up))
    inward_up = sum_over_xh(inward_up, xh, 0)
    outward_up = sum_along_y(outward_up, send_along_y(parts_along_y(outward_up, y)), y)
    rows_up, ahead_down_arrived, ahead_up_arrived = tie(
        (jnp.concatenate([inward_up, outward_up], axis=1), ahead_down_arrived, ahead_up_arrived)
    )
    from_mirror = mirror(rows_up.astype(jnp.bfloat16))
    rows_down = sum_over_xh(sum_along_y(total_down, y_down, y), xh, 0)
    down_out = section_forward(last_rows(0, ahead_down_arrived), matrix_down)
    up_out = section_forward(last_rows(1, ahead_up_arrived), matrix_up)
    total = rows_down + from_mirror.astype(jnp.float32)
    return jnp.stack([down_out, up_out])[:, None], total[None]


def solution(mesh):
    in_specs = (
        P(None, "dp", "section", None),
        P(None, "dp", None, None),
        P(None, "dp", "section", None),
        P(None, "dp", None, None),
        P(None, None, "dp", "section", None),
        P("section", "dp", None),
    )
    out_specs = (P(None, "dp", "section", None), P("section", "dp", None))
    return jax.shard_map(
        on_device, mesh=mesh, in_specs=in_specs, out_specs=out_specs, check_vma=False
    )
```

```python
import jax
import jax.numpy as jnp
from jax import lax
from jax.sharding import PartitionSpec as P

N_Y, N_XH, N_CORE = 4, 2, 2
ROWS = 128


def dp_index(y, xh, core):
    return (y & 3) << 2 | (xh & 1) << 1 | core & 1


def dp_coords(index):
    return index >> 2, index >> 1 & 1, index & 1


def dp_shift(block, dy=0, dxh=0, dcore=0):
    route = []
    for index in range(N_Y * N_XH * N_CORE):
        y, xh, core = dp_coords(index)
        route.append((index, dp_index(y + dy, xh + dxh, core + dcore)))
    return lax.ppermute(block, "dp", route)


def mirror(block):
    n = lax.axis_size("section")
    return lax.ppermute(block, "section", [(p, n - 1 - p) for p in range(n)])


def relay(block, step):
    n = lax.axis_size("section")
    return lax.ppermute(block, "section", [(p, p + step) for p in range(n) if 0 <= p + step < n])


def first_hops(shard):
    return dp_shift(shard, dy=-1), dp_shift(shard, dy=1)


def gather_half(shard, other, hops, y, xh, earlier):
    rows, width = shard.shape
    up, down = hops
    up_other, down_other = first_hops(other)
    up, down_other, earlier = lax.optimization_barrier((up, down_other, earlier))
    far = dp_shift(up, dy=-1)
    far_other = dp_shift(down_other, dy=1)
    half = jnp.zeros((N_Y * N_XH, rows, width), shard.dtype)
    for dy, dxh, block in (
        (0, 0, shard),
        (0, 1, other),
        (1, 0, up),
        (3, 0, down),
        (1, 1, up_other),
        (3, 1, down_other),
        (2, 0, far),
        (2, 1, far_other),
    ):
        place = (y + dy & 3) << 1 | xh ^ dxh
        half = lax.dynamic_update_slice(half, block[None], (place, 0, 0))
    return half, earlier


def interleaved(half, across, core):
    blocks, rows, width = half.shape
    even = core == 0
    pair = jnp.stack([jnp.where(even, half, across), jnp.where(even, across, half)], axis=1)
    return pair.reshape(N_CORE * blocks * rows, width)


def normalize(row_block):
    values = row_block.astype(jnp.float32)
    inverse = lax.rsqrt(jnp.mean(values * values, axis=-1, keepdims=True) + 1e-06)
    return values, inverse, (values * inverse).astype(jnp.bfloat16)


def gate_and_up(normed, matrix):
    width = matrix.shape[1] // 3
    projected = jnp.dot(normed, matrix[:, : 2 * width], preferred_element_type=jnp.float32)
    return projected[:, :width], projected[:, width:]


def project(row_block, matrix):
    values, inverse, normed = normalize(row_block)
    return values, inverse, normed, *gate_and_up(normed, matrix)


def section_forward(row_block, matrix):
    width = matrix.shape[1] // 3
    values, _, _, gate, up = project(row_block, matrix)
    hidden = (gate * jax.nn.sigmoid(gate) * up).astype(jnp.bfloat16)
    branch = lax.dot_general(
        hidden, matrix[:, 2 * width :], (((1,), (1,)), ((), ())), preferred_element_type=jnp.float32
    )
    return (values + branch).astype(jnp.bfloat16)


def hidden_of(gate, up):
    return (gate * jax.nn.sigmoid(gate) * up).astype(jnp.bfloat16)


def projected_grad_of(cotangent, gate, up, matrix):
    width = matrix.shape[1] // 3
    hidden_grad = jnp.dot(cotangent, matrix[:, 2 * width :], preferred_element_type=jnp.float32)
    sigmoid = jax.nn.sigmoid(gate)
    return jnp.concatenate(
        [
            hidden_grad * up * sigmoid * (1.0 + gate * (1.0 - sigmoid)),
            hidden_grad * (gate * sigmoid),
        ],
        axis=1,
    ).astype(jnp.bfloat16)


def input_grad_of(cotangent, values, inverse, projected_grad, matrix):
    width = matrix.shape[1] // 3
    normed_grad = lax.dot_general(
        projected_grad,
        matrix[:, : 2 * width],
        (((1,), (1,)), ((), ())),
        preferred_element_type=jnp.float32,
    )
    inner = jnp.mean(normed_grad * values, axis=-1, keepdims=True)
    return (
        cotangent.astype(jnp.float32)
        + inverse * normed_grad
        - values * inverse * inverse * inverse * inner
    ).astype(jnp.bfloat16)


def over_tokens(rows, grads):
    return lax.dot_general(rows, grads, (((0,), (0,)), ((), ())), preferred_element_type=jnp.float32)


def at(blocks, index, axis=0):
    return lax.dynamic_index_in_dim(blocks, index, axis=axis, keepdims=False)


def split_by_core(grad, core):
    halves = grad.reshape(-1, N_CORE, ROWS, grad.shape[1])
    return at(halves, core, 1), at(halves, 1 - core, 1)


def core_sum(own, arrived):
    sums = [a.astype(jnp.float32) + b.astype(jnp.float32) for a, b in zip(own, arrived)]
    total = jnp.concatenate(sums, axis=2).astype(jnp.bfloat16)
    return total.reshape(N_Y, N_XH, *total.shape[1:])


def parts_along_y(blocks, y):
    return [at(blocks, y + dy & 3) for dy in (1, 3, 2)]


def send_along_y(parts):
    return [dp_shift(part, dy=dy) for dy, part in zip((1, 3, 2), parts)]


def sum_along_y(blocks, arrived, y):
    total = at(blocks, y).astype(jnp.float32)
    for block in arrived:
        total = total + block.astype(jnp.float32)
    return total


def sum_over_xh(blocks, xh, axis):
    arrived = dp_shift(at(blocks, 1 - xh, axis).astype(jnp.bfloat16), dxh=1)
    return at(blocks, xh, axis).astype(jnp.float32) + arrived.astype(jnp.float32)


def on_device(
    block_arguments,
    incoming_batches,
    output_adjoints,
    objective_adjoints,
    kept_block_arguments,
    parameter_arrays,
):
    section = lax.axis_index("section")
    first = section == 0
    last = section == lax.axis_size("section") - 1
    y, xh, core = dp_coords(lax.axis_index("dp"))

    def joined(pair):
        return jnp.concatenate(pair, axis=0)

    ends = ((first, last), (last, first))
    tie = lax.optimization_barrier

    def first_tick(cotangent, matrix, norm):
        values, inverse, normed = norm
        gate, up = gate_and_up(normed, matrix)
        grad = projected_grad_of(cotangent, gate, up, matrix)
        back = input_grad_of(cotangent, values, inverse, grad, matrix)
        return (normed, grad, cotangent, hidden_of(gate, up)), back

    def second_tick(way, matrix, projected, back_arrived):
        normed, gate, up = projected
        cotangent = jnp.where(ends[way][1], objective_adjoints[way, 0], back_arrived)
        return normed, projected_grad_of(cotangent, gate, up, matrix), cotangent, hidden_of(gate, up)

    def rows_by_core(pieces_first, pieces_second):
        normed, grad, cotangent, hidden = (joined(pair) for pair in zip(pieces_first, pieces_second))
        inward = split_by_core(over_tokens(normed, grad).astype(jnp.bfloat16), core)
        outward = [
            split_by_core(over_tokens(cot, hidden).astype(jnp.bfloat16), core)
            for cot in jnp.split(cotangent, 2, axis=1)
        ]
        own, away = ([inward[k], joined([part[k] for part in outward])] for k in (0, 1))
        return own, away

    def core_swap(blocks):
        return [dp_shift(block, dcore=1) for block in blocks]

    def last_rows(way, ahead_arrived):
        return jnp.where(ends[way][0], incoming_batches[way, 0], ahead_arrived)

    own_shard = parameter_arrays[0]
    mirror_shard = mirror(own_shard)
    half_down, mirror_shard = gather_half(
        own_shard, dp_shift(own_shard, dxh=1), first_hops(own_shard), y, xh, mirror_shard
    )
    norm_down, norm_up = (normalize(kept_block_arguments[way, 0, 0]) for way in (0, 1))
    half_down, mirror_other, norm_down, cot_down, block_down = tie(
        (half_down, dp_shift(mirror_shard, dxh=1), norm_down, output_adjoints[0, 0], block_arguments[0, 0])
    )
    matrix_down = interleaved(half_down, dp_shift(half_down, dcore=1), core)
    down_first, back_down = first_tick(cot_down, matrix_down, norm_down)
    half_up, hidden_down = gather_half(
        mirror_shard, mirror_other, first_hops(mirror_shard), y, xh, down_first[3]
    )
    down_first = (*down_first[:3], hidden_down)
    back_down_arrived = relay(back_down, -1)
    across_up = dp_shift(half_up, dcore=1)
    ahead_down = section_forward(block_down, matrix_down)
    _, _, *projected_down = project(kept_block_arguments[0, 1, 0], matrix_down)
    back_down_arrived, ahead_down, projected_down = tie((back_down_arrived, ahead_down, projected_down))
    ahead_down_arrived = relay(ahead_down, 1)
    down_second = second_tick(0, matrix_down, projected_down, back_down_arrived)
    own_down, away_down = rows_by_core(down_first, down_second)

    half_up, across_up, away_down = tie((half_up, across_up, away_down))
    away_down_arrived = core_swap(away_down)
    matrix_up = interleaved(half_up, across_up, core)
    up_first, back_up = first_tick(output_adjoints[1, 0], matrix_up, norm_up)
    back_up, away_down_arrived = tie((back_up, away_down_arrived))
    back_up_arrived = relay(back_up, 1)
    total_down = core_sum(own_down, away_down_arrived)
    parts_down = parts_along_y(total_down, y)
    block_up, parts_down = tie((block_arguments[1, 0], parts_down))
    ahead_up = section_forward(block_up, matrix_up)
    _, _, *projected_up = project(kept_block_arguments[1, 1, 0], matrix_up)
    back_up_arrived, ahead_up, projected_up = tie((back_up_arrived, ahead_up, projected_up))
    ahead_up_arrived = relay(ahead_up, -1)
    up_second = second_tick(1, matrix_up, projected_up, back_up_arrived)
    own_up, away_up = rows_by_core(up_first, up_second)
    y_down = send_along_y(parts_down)
    away_up, y_down = tie((away_up, y_down))
    inward_up, outward_up = (core_sum([a], [b]) for a, b in zip(own_up, core_swap(away_up)))
    parts_up = parts_along_y(inward_up, y)
    outward_up = sum_over_xh(outward_up, xh, 1).astype(jnp.bfloat16)
    inward_up = sum_along_y(inward_up, send_along_y(parts_up), y)
    inward_up, outward_up, ahead_down_arrived, ahead_up_arrived = tie(
        (inward_up, outward_up, ahead_down_arrived, ahead_up_arrived)
    )
    inward_up = sum_over_xh(inward_up, xh, 0)
    outward_up = sum_along_y(outward_up, send_along_y(parts_along_y(outward_up, y)), y)
    rows_up = jnp.concatenate([inward_up, outward_up], axis=1)
    from_mirror = mirror(rows_up.astype(jnp.bfloat16))
    rows_down = sum_over_xh(sum_along_y(total_down, y_down, y), xh, 0)
    down_out = section_forward(last_rows(0, ahead_down_arrived), matrix_down)
    up_out = section_forward(last_rows(1, ahead_up_arrived), matrix_up)
    total = rows_down + from_mirror.astype(jnp.float32)
    return jnp.stack([down_out, up_out])[:, None], total[None]


def solution(mesh):
    in_specs = (
        P(None, "dp", "section", None),
        P(None, "dp", None, None),
        P(None, "dp", "section", None),
        P(None, "dp", None, None),
        P(None, None, "dp", "section", None),
        P("section", "dp", None),
    )
    out_specs = (P(None, "dp", "section", None), P("section", "dp", None))
    return jax.shard_map(
        on_device, mesh=mesh, in_specs=in_specs, out_specs=out_specs, check_vma=False
    )
```
